512 devices in a mesh: dp: 128 (over x, z, core), replica: 4 (over y).
Axes of the slice: x: 4, y: 4, z: 16, core: 2. Of those that a mesh axis runs over, the one named last changes fastest.
Arguments:
- gradient: float32 [8, 512, 27, 512], P(None, 'dp', None, 'replica'), may hold values from -1.2 to 1.2
- block_owner: int32 [216], replicated, may hold values from 0 to 127, as said below
- block_slab: int32 [216], replicated, may hold values from 0 to 7, as said below
- block_col: int32 [216], replicated, may hold values from 0 to 13312, as said below
- left_factor: float32 [384, 512, 512], P('dp', 'replica'), may hold values from -3 to 3
- right_factor: float32 [384, 512, 512], P('dp', 'replica'), may hold values from -3 to 3
- left_root: bfloat16 [384, 512, 512], P('dp', 'replica'), may hold values from -0.25 to 0.25
- right_root: bfloat16 [384, 512, 512], P('dp', None, 'replica'), may hold values from -0.25 to 0.25
Outputs:
- direction: float32 [8, 512, 27, 512], P(None, 'dp', None, 'replica')
- left_new: float32 [384, 512, 512], P('dp', 'replica')
- right_new: float32 [384, 512, 512], P('dp', 'replica')
The draws below stay inside these ranges and needn't reach their ends.
Inputs may be any that keep to these rules, and one draw needn't show every extreme that they name: `block_owner`: each owner is named by at most 3 entries, and some owner by exactly 3. block_slab and block_col together name every block of the gradient exactly once. `block_col`: a multiple of 512.
All inputs are finite; a program needn't handle non-finite values.
Results may differ from the reference program's by a relative error of at most 0.0003.
Values sent between devices are 32-bit elements; how exact they have to be, the bound alone decides.
No kernel may reach another device: no remote copies, remote signals or barrier semaphores. Data moves between devices by JAX's collectives and lax.ppermute only.
A program may use at most 64 MiB of HBM per device.

```python
import jax
import jax.numpy as jnp
from jax import lax

BS = 512
SLABS = 8
BCOLS = 27
BLOCKS = 216
CAP = 3
SLOTS = 384


def tile_order(key):
    return jax.random.permutation(jax.random.fold_in(key, 11), BLOCKS).astype(jnp.int32)


def draw_block_slab(key, part):
    order = tile_order(key)
    return (order // BCOLS).astype(jnp.int32)


def draw_block_col(key, part):
    order = tile_order(key)
    return (order % BCOLS * BS).astype(jnp.int32)


def draw_block_owner(key, part):
    key = jax.random.fold_in(key, 5)
    first_key, second_key, third_key = jax.random.split(key, 3)
    owner_count = SLOTS // CAP
    complete_block_owner = jax.random.randint(first_key, (), 0, owner_count).astype(jnp.int32)
    others = jax.random.permutation(second_key, (owner_count - 1) * CAP).astype(jnp.int32)
    picked = others[:BLOCKS - CAP] // CAP
    picked = picked + jnp.where(picked >= complete_block_owner, 1, 0).astype(jnp.int32)
    owners = jnp.concatenate([jnp.full((CAP,), 1, jnp.int32) * complete_block_owner, picked])
    shuffle = jax.random.permutation(third_key, BLOCKS)
    return owners[shuffle].astype(jnp.int32)


def steps_of(key, dims, cuts, low, high):
    factor_of, own = 1.0, jax.random.fold_in(key, 6)
    for dim, shards_of in cuts:
        draws = jnp.exp(jax.random.uniform(jax.random.fold_in(own, dim), (shards_of,), jnp.float32, low / len(cuts), high / len(cuts)))
        factor_of = factor_of * jnp.repeat(draws, dims[dim] // shards_of).reshape([-1 if axis == dim else 1 for axis in range(len(dims))])
    return factor_of


def bell_draw(stream_key, shape, spread, bound, cuts=(), kind=jnp.bfloat16):
    drawn = jax.random.normal(stream_key, shape, jnp.float32) * spread
    if len(cuts) > 0:
        drawn = steps_of(stream_key, shape, cuts, -0.22, 0.18) * drawn
    return jnp.clip(drawn, min=-bound, max=bound).astype(kind)


def setup_inputs(seed: int = 0) -> dict:
    seeds = jax.random.split(jax.random.key(seed), 9)
    return {
        "gradient": bell_draw(seeds[0], (SLABS, BS, BCOLS, BS), 0.2, 1.2, ((1, 128), (3, 4)), jnp.float32),
        "block_owner": draw_block_owner(jax.random.fold_in(seeds[8], 71), 0),
        "block_slab": draw_block_slab(jax.random.fold_in(seeds[8], 71), 0),
        "block_col": draw_block_col(jax.random.fold_in(seeds[8], 71), 0),
        "left_factor": bell_draw(seeds[4], (SLOTS, BS, BS), 0.5, 3.0, ((0, 128), (1, 4)), jnp.float32),
        "right_factor": bell_draw(seeds[5], (SLOTS, BS, BS), 0.5, 3.0, ((0, 128), (1, 4)), jnp.float32),
        "left_root": bell_draw(seeds[6], (SLOTS, BS, BS), BS ** -0.5, 0.25, ((0, 128), (1, 4))),
        "right_root": bell_draw(seeds[7], (SLOTS, BS, BS), BS ** -0.5, 0.25, ((0, 128), (2, 4))),
    }


BETA = 0.95


def reference(gradient, block_owner, block_slab, block_col, left_factor, right_factor, left_root, right_root):
    position = jnp.arange(BLOCKS, dtype=jnp.int32)
    earlier = position[None, :] < position[:, None]
    same_owner = block_owner[:, None] == block_owner[None, :]
    slot_rank = jnp.sum(jnp.where(earlier & same_owner, 1, 0), axis=1).astype(jnp.int32)
    slot_of_block = (block_owner * CAP + slot_rank).astype(jnp.int32)
    block_index = (block_col // BS).astype(jnp.int32)
    blocks = gradient[block_slab, :, block_index, :]
    left_statistic_matrix = jnp.einsum("kab,kcb->kac", blocks, blocks, precision=lax.Precision.HIGHEST)
    right_gram = jnp.einsum("kab,kac->kbc", blocks, blocks, precision=lax.Precision.HIGHEST)
    left_new = (BETA * left_factor).at[slot_of_block].set(BETA * left_factor[slot_of_block] + (1.0 - BETA) * left_statistic_matrix)
    right_new = (BETA * right_factor).at[slot_of_block].set(BETA * right_factor[slot_of_block] + (1.0 - BETA) * right_gram)
    left_used = left_root[slot_of_block].astype(jnp.float32)
    right_used = right_root[slot_of_block].astype(jnp.float32)
    products = jnp.einsum("kab,kbc->kac", left_used, blocks, precision=lax.Precision.HIGHEST)
    directions = jnp.einsum("kab,kbc->kac", products, right_used, precision=lax.Precision.HIGHEST)
    tile_of_block = (block_slab * BCOLS + block_index).astype(jnp.int32)
    placed = jnp.zeros((SLABS * BCOLS, BS, BS), directions.dtype).at[tile_of_block].set(directions)
    direction = placed.reshape(SLABS, BCOLS, BS, BS).transpose(0, 2, 1, 3)
    return direction, left_new, right_new
```

```python
import functools

import jax
import jax.numpy as jnp
from jax import lax
from jax.experimental import pallas as pl
from jax.experimental.pallas import tpu as pltpu
from jax.sharding import Mesh
from jax.sharding import PartitionSpec as P

BETA = 0.95
STRIDE = 32
VMEM_BYTES = 24 * 1024 * 1024
F32 = jnp.float32
BF16 = jnp.bfloat16
SMEM_SPEC = pl.BlockSpec(memory_space=pltpu.SMEM)
VMEM_SPEC = pl.BlockSpec(memory_space=pltpu.VMEM)


def call(body, name, out_shape, out_specs, in_specs, scratch=(), flops=0, moved=1_000_000, vmem=VMEM_BYTES):
    return pl.pallas_call(
        body,
        out_shape=out_shape,
        in_specs=in_specs,
        out_specs=out_specs,
        scratch_shapes=list(scratch),
        compiler_params=pltpu.CompilerParams(vmem_limit_bytes=vmem),
        cost_estimate=pl.CostEstimate(flops=flops, bytes_accessed=moved, transcendentals=0),
        name=name,
    )


def log2(size):
    return size.bit_length() - 1


def capacities(plane_slots):
    return sorted({plane_slots * 3 // 4, plane_slots * 5 // 6, plane_slots})


def select_kernel(sizes, owner_hbm, slab_hbm, col_hbm, grad_hbm, *refs):
    blocks, owners, cap, x_size, z_size, core_size, y_size, cols, side = sizes
    tiers = capacities(x_size * core_size * cap)
    send_refs, refs = refs[: len(tiers)], refs[len(tiers) :]
    plan_ref, tier_ref, owner_ref, slab_ref, col_ref, grad_ref, pack_ref = refs[:7]
    count_ref, fill_ref, sems = refs[7:]
    stride = pack_ref.shape[1]
    copies = [
        pltpu.make_async_copy(source, target, sems.at[i])
        for i, (source, target) in enumerate(
            ((owner_hbm, owner_ref), (slab_hbm, slab_ref), (col_hbm, col_ref), (grad_hbm, grad_ref))
        )
    ]
    for copy in copies:
        copy.start()

    def clear(o, carry):
        count_ref[o] = 0
        return carry

    lax.fori_loop(0, owners, clear, 0, unroll=16)
    for z in range(z_size):
        fill_ref[z] = 0
    for s in range(stride):
        plan_ref[blocks + s] = y_size - 1
    plan_ref[blocks + 2 * stride] = lax.axis_index("y")
    z_here = lax.axis_index("z")
    for copy in copies:
        copy.wait()

    def move(k, carry):
        o = owner_ref[k]
        rank = count_ref[o]
        count_ref[o] = rank + 1
        core = o & (core_size - 1)
        z = (o >> log2(core_size)) & (z_size - 1)
        x = o >> (log2(core_size) + log2(z_size))
        spot = fill_ref[z]
        fill_ref[z] = spot + 1
        tile = slab_ref[k] * cols + (col_ref[k] >> log2(side))
        plan_ref[tile] = z * stride + spot
        slot = (x * core_size + core) * y_size + rank
        plan_ref[spot + jnp.where(z == z_here, blocks, blocks + stride)] = slot
        pack_ref[z, spot] = grad_ref[tile]
        return carry

    lax.fori_loop(0, blocks, move, 0, unroll=24)
    most = fill_ref[0]
    for z in range(1, z_size):
        most = jnp.maximum(most, fill_ref[z])
    tier = jnp.int32(len(tiers) - 1)
    for i in range(len(tiers) - 2, -1, -1):
        tier = jnp.where(most <= tiers[i], i, tier)
    tier_ref[0] = tier
    for i, send_ref in enumerate(send_refs):

        @pl.when(tier == i)
        def _():
            copy = pltpu.make_async_copy(pack_ref.at[:, : tiers[i]], send_ref, sems.at[4])
            copy.start()
            copy.wait()


def place_kernel(plan_ref, back_ref, out_ref):
    bits = log2(STRIDE)

    def step(t, carry):
        code = plan_ref[t]
        out_ref[t] = back_ref[code >> bits, code & (STRIDE - 1)]
        return carry

    lax.fori_loop(0, out_ref.shape[0], step, 0, unroll=8)


def forward_kernel(cap, blocks, plan_ref, in_ref, *refs):
    out_ref = refs[-1]
    planes, y_size = out_ref.shape[:2]
    for p in range(planes):
        out_ref[p, :cap] = jnp.zeros_like(out_ref[p, :cap])
    for spot in range(in_ref.shape[1]):
        slot = plan_ref[blocks + spot]
        out_ref[slot >> log2(y_size), slot & (y_size - 1)] = in_ref[:, spot]


def backward_kernel(blocks, plan_ref, in_ref, after_ref, out_ref):
    y_size = in_ref.shape[1]
    for spot in range(out_ref.shape[1]):
        slot = plan_ref[blocks + spot]
        out_ref[:, spot] = in_ref[slot >> log2(y_size), slot & (y_size - 1)]


def around(position, size):
    return position & (size - 1)


def roots_kernel(plan_ref, left_ref, right_ref, *out_refs):
    parts = len(out_refs)
    quarter = left_ref.shape[1]
    for d, out_ref in enumerate(out_refs):
        s = jnp.minimum(around(plan_ref[plan_ref.shape[0] - 1] + d, parts), left_ref.shape[0] - 1)
        left = left_ref[s].astype(F32)
        right = right_ref[s].astype(F32)
        for j in range(parts):
            out_ref[j] = left[:, j * quarter : (j + 1) * quarter]
            out_ref[parts + j] = right[j * quarter : (j + 1) * quarter]


def split(value):
    high = value.astype(BF16)
    return high, (value - high.astype(F32)).astype(BF16)


def dot(a, b, a_dim, b_dim):
    return lax.dot_general(a, b, (((a_dim,), (b_dim,)), ((), ())), preferred_element_type=F32)


def direction_kernel(plan_ref, in_ref, *refs):
    x_size, core_size, parts, z_size, rows, width = in_ref.shape
    pieces, (out_ref, block_ref, left_ref, right_ref, result_ref) = refs[:parts], refs[parts:]
    side = parts * width
    for x in range(x_size):
        for c in range(core_size):
            for q in range(parts):
                block_ref[
                    x * z_size : (x + 1) * z_size, c * rows : (c + 1) * rows, q * width : (q + 1) * width
                ] = in_ref[x, c, q]
    for d, piece in enumerate(pieces):
        q = around(plan_ref[plan_ref.shape[0] - 1] - d, parts)
        for j in range(parts):
            left_ref[pl.ds(q * width, width), j * width : (j + 1) * width] = piece[j].astype(BF16)
            right_ref[q, j * width : (j + 1) * width, :] = piece[parts + j].astype(BF16)
    high, low = split(block_ref[...].reshape(side, side))
    right = jnp.concatenate([right_ref[q] for q in range(parts)], axis=1)
    product = dot(high, right, 1, 0) + dot(low, right, 1, 0)
    high, low = split(product)
    left = left_ref[...]
    result_ref[...] = (dot(left, high, 1, 0) + dot(left, low, 1, 0)).reshape(result_ref.shape)
    for x in range(x_size):
        for c in range(core_size):
            for q in range(parts):
                out_ref[x, c, q] = result_ref[
                    x * z_size : (x + 1) * z_size, c * rows : (c + 1) * rows, q * width : (q + 1) * width
                ]


def grams_kernel(plan_ref, block_ref, *refs):
    out_refs, gram_ref = refs[:-1], refs[-1]
    parts = len(out_refs)
    quarter = out_refs[0].shape[1]
    side = block_ref.shape[2]
    high, low = split(block_ref[...].reshape(side, side))
    for i, dim in enumerate((1, 0)):
        gram_ref[i] = dot(high, high, dim, dim) + (dot(high, low, dim, dim) + dot(low, high, dim, dim))
    for d, out_ref in enumerate(out_refs):
        q = around(plan_ref[plan_ref.shape[0] - 1] + d, parts)
        out_ref[...] = gram_ref[:, pl.ds(q * quarter, quarter), :]


def factors_kernel(plan_ref, after_ref, left_ref, right_ref, *refs):
    pieces, (left_out, right_out) = refs[:-2], refs[-2:]
    for d, piece in enumerate(pieces):
        s = around(plan_ref[plan_ref.shape[0] - 1] - d, len(pieces))

        @pl.when(s < left_ref.shape[0])
        def _():
            left_out[s] = BETA * left_ref[s] + (1.0 - BETA) * piece[0]
            right_out[s] = BETA * right_ref[s] + (1.0 - BETA) * piece[1]


def exchange(value, axes):
    return lax.all_to_all(value, axes, split_axis=0, concat_axis=0, tiled=True)


def spread(pieces):
    size = len(pieces)
    turn = lambda d: [(i, (i + d) % size) for i in range(size)]
    return [pieces[0]] + [lax.ppermute(pieces[d], "y", turn(d)) for d in range(1, size)]


def shape(*dims):
    return jax.ShapeDtypeStruct(dims, F32)


def step(index, blocks, plan, sends, left_factor, right_factor, left_root, right_root):
    x_size, z_size = lax.axis_size("x"), lax.axis_size("z")
    core_size, y_size = lax.axis_size("core"), lax.axis_size("y")
    planes = x_size * core_size
    cap, quarter, side = left_factor.shape
    send = sends[index]
    _, capacity, rows, width = send.shape
    cube = side * side * side * 2

    roots = spread(
        call(
            roots_kernel,
            "roots",
            (shape(2 * y_size, quarter, quarter),) * y_size,
            (VMEM_SPEC,) * y_size,
            [SMEM_SPEC, VMEM_SPEC, VMEM_SPEC],
        )(plan, left_root, right_root)
    )

    moved = exchange(send, "z")
    moved = call(
        functools.partial(forward_kernel, cap, blocks),
        "forward",
        shape(planes, y_size, z_size, rows, width),
        VMEM_SPEC,
        [SMEM_SPEC, VMEM_SPEC] + [pl.BlockSpec(memory_space=pl.ANY)] * y_size,
    )(plan, moved, *roots)
    moved = exchange(moved.reshape(planes * y_size, z_size, rows, width), ("x", "core", "y"))

    directions, block = call(
        direction_kernel,
        "direction",
        (
            shape(x_size, core_size, y_size, z_size, rows, width),
            pltpu.HBM((x_size * z_size, core_size * rows, side), F32),
        ),
        (VMEM_SPEC, VMEM_SPEC),
        [SMEM_SPEC, VMEM_SPEC] + [VMEM_SPEC] * y_size,
        [
            pltpu.VMEM((side, side), BF16),
            pltpu.VMEM((y_size, side, width), BF16),
            pltpu.VMEM((x_size * z_size, core_size * rows, side), F32),
        ],
        flops=4 * cube,
        moved=6_000_000,
    )(plan, moved.reshape(x_size, core_size, y_size, z_size, rows, width), *roots)

    grams = spread(
        call(
            grams_kernel,
            "grams",
            (shape(2, quarter, side),) * y_size,
            (VMEM_SPEC,) * y_size,
            [SMEM_SPEC, VMEM_SPEC],
            [pltpu.VMEM((2, side, side), F32)],
            flops=6 * cube,
            moved=5_000_000,
        )(plan, block)
    )
    back = exchange(directions.reshape(planes * y_size, z_size, rows, width), ("x", "core", "y"))
    back = call(
        functools.partial(backward_kernel, blocks),
        "backward",
        shape(z_size, capacity, rows, width),
        VMEM_SPEC,
        [SMEM_SPEC, VMEM_SPEC, pl.BlockSpec(memory_space=pl.ANY)],
    )(plan, back.reshape(planes, y_size, z_size, rows, width), grams[0])
    back = exchange(back, "z")

    result = pltpu.HBM((blocks, rows, width), F32)
    placed = call(place_kernel, "place", result, VMEM_SPEC, [SMEM_SPEC, VMEM_SPEC])(
        plan, back
    )
    left_new, right_new = call(
        factors_kernel,
        "factors",
        (shape(*left_factor.shape), shape(*right_factor.shape)),
        (VMEM_SPEC, VMEM_SPEC),
        [SMEM_SPEC, pl.BlockSpec(memory_space=pl.ANY)] + [VMEM_SPEC] * (2 + y_size),
        moved=5_000_000,
    )(plan, placed, left_factor, right_factor, *grams)

    return placed, left_new, right_new


def per_device(
    gradient, block_owner, block_slab, block_col, left_factor, right_factor, left_root, right_root
):
    x_size, z_size = lax.axis_size("x"), lax.axis_size("z")
    core_size, y_size = lax.axis_size("core"), lax.axis_size("y")
    owners = x_size * z_size * core_size
    cap, quarter, side = left_factor.shape
    slabs, rows, cols, width = gradient.shape
    blocks = block_owner.shape[0]
    tiers = capacities(x_size * core_size * cap)
    assert tiers[-1] <= STRIDE and cap < y_size
    index = lambda size: jax.ShapeDtypeStruct((size,), jnp.int32)
    any_spec = pl.BlockSpec(memory_space=pl.ANY)

    sizes = (blocks, owners, cap, x_size, z_size, core_size, y_size, cols, side)
    *sends, plan, tier = call(
        functools.partial(select_kernel, sizes),
        "select",
        tuple(shape(z_size, capacity, rows, width) for capacity in tiers)
        + (index(blocks + 2 * STRIDE + 1), index(1)),
        (any_spec,) * len(tiers) + (SMEM_SPEC,) * 2,
        [any_spec] * 4,
        [pltpu.SMEM((blocks,), jnp.int32)] * 3
        + [pltpu.VMEM((blocks, rows, width), F32), pltpu.VMEM((z_size, STRIDE, rows, width), F32)]
        + [pltpu.SMEM((owners,), jnp.int32), pltpu.SMEM((z_size,), jnp.int32), pltpu.SemaphoreType.DMA((5,))],
        moved=3_000_000,
        vmem=63 * 1024 * 1024,
    )(
        block_owner,
        block_slab,
        block_col,
        gradient.transpose(0, 2, 1, 3).reshape(blocks, rows, width),
    )
    placed, left_new, right_new = lax.switch(
        tier[0],
        [functools.partial(step, i, blocks) for i in range(len(tiers))],
        plan,
        sends,
        left_factor,
        right_factor,
        left_root,
        right_root,
    )
    placed = placed.reshape(slabs, cols, rows, width).transpose(0, 2, 1, 3)
    return placed, left_new, right_new


def solution(mesh, sizes=(4, 16, 2, 4)):
    fine = Mesh(mesh.devices.reshape(sizes), ("x", "z", "core", "y"))
    dp = ("x", "z", "core")
    return jax.shard_map(
        per_device,
        mesh=fine,
        in_specs=(
            P(None, dp, None, "y"),
            P(),
            P(),
            P(),
            P(dp, "y", None),
            P(dp, "y", None),
            P(dp, "y", None),
            P(dp, None, "y"),
        ),
        out_specs=(P(None, dp, None, "y"), P(dp, "y", None), P(dp, "y", None)),
        check_vma=False,
    )
```

```python
import functools

import jax
import jax.numpy as jnp
from jax import lax
from jax.experimental import pallas as pl
from jax.experimental.pallas import tpu as pltpu
from jax.sharding import Mesh
from jax.sharding import PartitionSpec as P

BETA = 0.95
STRIDE = 32
VMEM_BYTES = 24 * 1024 * 1024
F32 = jnp.float32
BF16 = jnp.bfloat16
SMEM_SPEC = pl.BlockSpec(memory_space=pltpu.SMEM)
VMEM_SPEC = pl.BlockSpec(memory_space=pltpu.VMEM)


def call(body, name, out_shape, out_specs, in_specs, scratch=(), flops=0, moved=1_000_000, vmem=VMEM_BYTES):
    return pl.pallas_call(
        body,
        out_shape=out_shape,
        in_specs=in_specs,
        out_specs=out_specs,
        scratch_shapes=list(scratch),
        compiler_params=pltpu.CompilerParams(vmem_limit_bytes=vmem),
        cost_estimate=pl.CostEstimate(flops=flops, bytes_accessed=moved, transcendentals=0),
        name=name,
    )


def log2(size):
    return size.bit_length() - 1


def capacities(plane_slots):
    return sorted({plane_slots * 3 // 4, plane_slots * 5 // 6, plane_slots})


def select_kernel(sizes, owner_hbm, slab_hbm, col_hbm, grad_hbm, *refs):
    blocks, owners, cap, x_size, z_size, core_size, y_size, cols, side = sizes
    tiers = capacities(x_size * core_size * cap)
    send_refs, refs = refs[: len(tiers)], refs[len(tiers) :]
    plan_ref, tier_ref, owner_ref, slab_ref, col_ref, grad_ref, pack_ref = refs[:7]
    count_ref, fill_ref, sems = refs[7:]
    stride = pack_ref.shape[1]
    copies = [
        pltpu.make_async_copy(source, target, sems.at[i])
        for i, (source, target) in enumerate(
            ((owner_hbm, owner_ref), (slab_hbm, slab_ref), (col_hbm, col_ref), (grad_hbm, grad_ref))
        )
    ]
    for copy in copies:
        copy.start()

    def clear(o, carry):
        count_ref[o] = 0
        return carry

    lax.fori_loop(0, owners, clear, 0, unroll=16)
    for z in range(z_size):
        fill_ref[z] = 0
    for s in range(stride):
        plan_ref[blocks + s] = y_size - 1
    plan_ref[blocks + 2 * stride] = lax.axis_index("y")
    z_here = lax.axis_index("z")
    for copy in copies:
        copy.wait()

    def move(k, carry):
        o = owner_ref[k]
        rank = count_ref[o]
        count_ref[o] = rank + 1
        core = o & (core_size - 1)
        z = (o >> log2(core_size)) & (z_size - 1)
        x = o >> (log2(core_size) + log2(z_size))
        spot = fill_ref[z]
        fill_ref[z] = spot + 1
        tile = slab_ref[k] * cols + (col_ref[k] >> log2(side))
        plan_ref[tile] = z * stride + spot
        slot = (x * core_size + core) * y_size + rank
        plan_ref[spot + jnp.where(z == z_here, blocks, blocks + stride)] = slot
        pack_ref[z, spot] = grad_ref[tile]
        return carry

    lax.fori_loop(0, blocks, move, 0, unroll=24)
    most = fill_ref[0]
    for z in range(1, z_size):
        most = jnp.maximum(most, fill_ref[z])
    tier = jnp.int32(len(tiers) - 1)
    for i in range(len(tiers) - 2, -1, -1):
        tier = jnp.where(most <= tiers[i], i, tier)
    tier_ref[0] = tier
    for i, send_ref in enumerate(send_refs):

        @pl.when(tier == i)
        def _():
            copy = pltpu.make_async_copy(pack_ref.at[:, : tiers[i]], send_ref, sems.at[4])
            copy.start()
            copy.wait()


def forward_kernel(cap, blocks, plan_ref, in_ref, *refs):
    out_ref = refs[-1]
    planes, y_size = out_ref.shape[:2]
    for p in range(planes):
        out_ref[p, :cap] = jnp.zeros_like(out_ref[p, :cap])
    for spot in range(in_ref.shape[1]):
        slot = plan_ref[blocks + spot]
        out_ref[slot >> log2(y_size), slot & (y_size - 1)] = in_ref[:, spot]


def backward_kernel(blocks, plan_ref, in_ref, after_ref, out_ref):
    y_size = in_ref.shape[1]
    for spot in range(out_ref.shape[1]):
        slot = plan_ref[blocks + spot]
        out_ref[:, spot] = in_ref[slot >> log2(y_size), slot & (y_size - 1)]


def around(position, size):
    return position & (size - 1)


def roots_kernel(plan_ref, left_ref, right_ref, *out_refs):
    parts = len(out_refs)
    quarter = left_ref.shape[1]
    for d, out_ref in enumerate(out_refs):
        s = jnp.minimum(around(plan_ref[plan_ref.shape[0] - 1] + d, parts), left_ref.shape[0] - 1)
        left = left_ref[s].astype(F32)
        right = right_ref[s].astype(F32)
        for j in range(parts):
            out_ref[j] = left[:, j * quarter : (j + 1) * quarter]
            out_ref[parts + j] = right[j * quarter : (j + 1) * quarter]


def split(value):
    high = value.astype(BF16)
    return high, (value - high.astype(F32)).astype(BF16)


def dot(a, b, a_dim, b_dim):
    return lax.dot_general(a, b, (((a_dim,), (b_dim,)), ((), ())), preferred_element_type=F32)


def tiles(shape):
    x_size, core_size, parts, z_size, rows, width = shape
    for x in range(x_size):
        for c in range(core_size):
            for q in range(parts):
                spot = (slice(x * z_size, (x + 1) * z_size), slice(c * rows, (c + 1) * rows))
                yield (x, c, q), spot + (slice(q * width, (q + 1) * width),)


def direction_kernel(plan_ref, in_ref, *refs):
    parts, width = in_ref.shape[2], in_ref.shape[5]
    pieces, (out_ref, block_ref, left_ref, right_ref, result_ref) = refs[:parts], refs[parts:]
    side = parts * width
    for part, spot in tiles(in_ref.shape):
        block_ref[spot] = in_ref[part]
    for d, piece in enumerate(pieces):
        q = around(plan_ref[plan_ref.shape[0] - 1] - d, parts)
        for j in range(parts):
            left_ref[pl.ds(q * width, width), j * width : (j + 1) * width] = piece[j].astype(BF16)
            right_ref[q, j * width : (j + 1) * width, :] = piece[parts + j].astype(BF16)
    high, low = split(block_ref[...].reshape(side, side))
    right = jnp.concatenate([right_ref[q] for q in range(parts)], axis=1)
    product = dot(high, right, 1, 0) + dot(low, right, 1, 0)
    high, low = split(product)
    left = left_ref[...]
    result_ref[...] = (dot(left, high, 1, 0) + dot(left, low, 1, 0)).reshape(result_ref.shape)
    for part, spot in tiles(in_ref.shape):
        out_ref[part] = result_ref[spot]


def grams_kernel(plan_ref, in_ref, after_ref, *refs):
    out_refs, (block_ref, gram_ref) = refs[:-2], refs[-2:]
    parts = len(out_refs)
    quarter = out_refs[0].shape[1]
    side = block_ref.shape[2]
    for part, spot in tiles(in_ref.shape):
        block_ref[spot] = in_ref[part]
    high, low = split(block_ref[...].reshape(side, side))
    for i, dim in enumerate((1, 0)):
        gram_ref[i] = dot(high, high, dim, dim) + (dot(high, low, dim, dim) + dot(low, high, dim, dim))
    for d, out_ref in enumerate(out_refs):
        q = around(plan_ref[plan_ref.shape[0] - 1] + d, parts)
        out_ref[...] = gram_ref[:, pl.ds(q * quarter, quarter), :]


def finish_kernel(plan_ref, back_ref, left_hbm, right_hbm, *refs):
    parts = len(refs) - 7
    pieces, refs = refs[:parts], refs[parts:]
    placed_hbm, left_out, right_out, placed_ref, left_ref, right_ref, sems = refs
    blocks = placed_ref.shape[0]
    bits = log2(STRIDE)
    loads = [
        pltpu.make_async_copy(left_hbm, left_ref, sems.at[0]),
        pltpu.make_async_copy(right_hbm, right_ref, sems.at[1]),
    ]
    for copy in loads:
        copy.start()

    def step(t, carry):
        code = plan_ref[t]
        placed_ref[t] = back_ref[code >> bits, code & (STRIDE - 1)]
        return carry

    lax.fori_loop(0, blocks, step, 0, unroll=8)
    stores = [
        pltpu.make_async_copy(placed_ref, placed_hbm, sems.at[2]),
        pltpu.make_async_copy(left_ref, left_out, sems.at[3]),
        pltpu.make_async_copy(right_ref, right_out, sems.at[4]),
    ]
    stores[0].start()
    for i, ref in enumerate((left_ref, right_ref)):
        loads[i].wait()
        for d, piece in enumerate(pieces):
            s = around(plan_ref[plan_ref.shape[0] - 1] - d, parts)

            @pl.when(s < ref.shape[0])
            def _():
                ref[s] = BETA * ref[s] + (1.0 - BETA) * piece[i]

        stores[1 + i].start()
    for copy in stores:
        copy.wait()


def exchange(value, axes):
    return lax.all_to_all(value, axes, split_axis=0, concat_axis=0, tiled=True)


def spread(pieces):
    size = len(pieces)
    turn = lambda d: [(i, (i + d) % size) for i in range(size)]
    return [pieces[0]] + [lax.ppermute(pieces[d], "y", turn(d)) for d in range(1, size)]


def shape(*dims):
    return jax.ShapeDtypeStruct(dims, F32)


def step(index, blocks, plan, sends, left_factor, right_factor, left_root, right_root):
    x_size, z_size = lax.axis_size("x"), lax.axis_size("z")
    core_size, y_size = lax.axis_size("core"), lax.axis_size("y")
    planes = x_size * core_size
    cap, quarter, side = left_factor.shape
    send = sends[index]
    _, capacity, rows, width = send.shape
    cube = side * side * side * 2
    any_spec = pl.BlockSpec(memory_space=pl.ANY)

    roots = spread(
        call(
            roots_kernel,
            "roots",
            (shape(2 * y_size, quarter, quarter),) * y_size,
            (VMEM_SPEC,) * y_size,
            [SMEM_SPEC, VMEM_SPEC, VMEM_SPEC],
        )(plan, left_root, right_root)
    )

    moved = exchange(send, "z")
    moved = call(
        functools.partial(forward_kernel, cap, blocks),
        "forward",
        shape(planes, y_size, z_size, rows, width),
        VMEM_SPEC,
        [SMEM_SPEC, VMEM_SPEC] + [pl.BlockSpec(memory_space=pl.ANY)] * y_size,
    )(plan, moved, *roots)
    moved = exchange(moved.reshape(planes * y_size, z_size, rows, width), ("x", "core", "y"))

    moved = moved.reshape(x_size, core_size, y_size, z_size, rows, width)
    whole = pltpu.VMEM((x_size * z_size, core_size * rows, side), F32)
    directions = call(
        direction_kernel,
        "direction",
        shape(*moved.shape),
        VMEM_SPEC,
        [SMEM_SPEC, VMEM_SPEC] + [VMEM_SPEC] * y_size,
        [
            whole,
            pltpu.VMEM((side, side), BF16),
            pltpu.VMEM((y_size, side, width), BF16),
            whole,
        ],
        flops=4 * cube,
        moved=6_000_000,
    )(plan, moved, *roots)

    grams = spread(
        call(
            grams_kernel,
            "grams",
            (shape(2, quarter, side),) * y_size,
            (VMEM_SPEC,) * y_size,
            [SMEM_SPEC, VMEM_SPEC, any_spec],
            [whole, pltpu.VMEM((2, side, side), F32)],
            flops=6 * cube,
            moved=5_000_000,
        )(plan, moved, directions)
    )
    back = exchange(directions.reshape(planes * y_size, z_size, rows, width), ("x", "core", "y"))
    back = call(
        functools.partial(backward_kernel, blocks),
        "backward",
        shape(z_size, capacity, rows, width),
        VMEM_SPEC,
        [SMEM_SPEC, VMEM_SPEC, pl.BlockSpec(memory_space=pl.ANY)],
    )(plan, back.reshape(planes, y_size, z_size, rows, width), grams[0])
    back = exchange(back, "z")

    factor = pltpu.VMEM(left_factor.shape, F32)
    return call(
        finish_kernel,
        "finish",
        (shape(blocks, rows, width), shape(*left_factor.shape), shape(*right_factor.shape)),
        (any_spec,) * 3,
        [SMEM_SPEC, VMEM_SPEC, any_spec, any_spec] + [VMEM_SPEC] * y_size,
        [pltpu.VMEM((blocks, rows, width), F32), factor, factor, pltpu.SemaphoreType.DMA((5,))],
        moved=6_000_000,
    )(plan, back, left_factor, right_factor, *grams)


def per_device(
    gradient, block_owner, block_slab, block_col, left_factor, right_factor, left_root, right_root
):
    x_size, z_size = lax.axis_size("x"), lax.axis_size("z")
    core_size, y_size = lax.axis_size("core"), lax.axis_size("y")
    owners = x_size * z_size * core_size
    cap, quarter, side = left_factor.shape
    slabs, rows, cols, width = gradient.shape
    blocks = block_owner.shape[0]
    tiers = capacities(x_size * core_size * cap)
    assert tiers[-1] <= STRIDE and cap < y_size
    index = lambda size: jax.ShapeDtypeStruct((size,), jnp.int32)
    any_spec = pl.BlockSpec(memory_space=pl.ANY)

    sizes = (blocks, owners, cap, x_size, z_size, core_size, y_size, cols, side)
    *sends, plan, tier = call(
        functools.partial(select_kernel, sizes),
        "select",
        tuple(shape(z_size, capacity, rows, width) for capacity in tiers)
        + (index(blocks + 2 * STRIDE + 1), index(1)),
        (any_spec,) * len(tiers) + (SMEM_SPEC,) * 2,
        [any_spec] * 4,
        [pltpu.SMEM((blocks,), jnp.int32)] * 3
        + [pltpu.VMEM((blocks, rows, width), F32), pltpu.VMEM((z_size, STRIDE, rows, width), F32)]
        + [pltpu.SMEM((owners,), jnp.int32), pltpu.SMEM((z_size,), jnp.int32), pltpu.SemaphoreType.DMA((5,))],
        moved=3_000_000,
        vmem=63 * 1024 * 1024,
    )(
        block_owner,
        block_slab,
        block_col,
        gradient.transpose(0, 2, 1, 3).reshape(blocks, rows, width),
    )
    placed, left_new, right_new = lax.switch(
        tier[0],
        [functools.partial(step, i, blocks) for i in range(len(tiers))],
        plan,
        sends,
        left_factor,
        right_factor,
        left_root,
        right_root,
    )
    placed = placed.reshape(slabs, cols, rows, width).transpose(0, 2, 1, 3)
    return placed, left_new, right_new


def solution(mesh, sizes=(4, 16, 2, 4)):
    fine = Mesh(mesh.devices.reshape(sizes), ("x", "z", "core", "y"))
    dp = ("x", "z", "core")
    return jax.shard_map(
        per_device,
        mesh=fine,
        in_specs=(
            P(None, dp, None, "y"),
            P(),
            P(),
            P(),
            P(dp, "y", None),
            P(dp, "y", None),
            P(dp, "y", None),
            P(dp, None, "y"),
        ),
        out_specs=(P(None, dp, None, "y"), P(dp, "y", None), P(dp, "y", None)),
        check_vma=False,
    )
```

```python
import functools

import jax
import jax.numpy as jnp
from jax import lax
from jax.experimental import pallas as pl
from jax.experimental.pallas import tpu as pltpu
from jax.sharding import Mesh
from jax.sharding import PartitionSpec as P

BETA = 0.95
STRIDE = 32
VMEM_BYTES = 24 * 1024 * 1024
F32 = jnp.float32
BF16 = jnp.bfloat16
SMEM_SPEC = pl.BlockSpec(memory_space=pltpu.SMEM)
VMEM_SPEC = pl.BlockSpec(memory_space=pltpu.VMEM)


def call(body, name, out_shape, out_specs, in_specs, scratch=(), flops=0, moved=1_000_000, vmem=VMEM_BYTES):
    return pl.pallas_call(
        body,
        out_shape=out_shape,
        in_specs=in_specs,
        out_specs=out_specs,
        scratch_shapes=list(scratch),
        compiler_params=pltpu.CompilerParams(vmem_limit_bytes=vmem),
        cost_estimate=pl.CostEstimate(flops=flops, bytes_accessed=moved, transcendentals=0),
        name=name,
    )


def log2(size):
    return size.bit_length() - 1


def capacities(plane_slots):
    return sorted({plane_slots * 3 // 4, plane_slots * 5 // 6, plane_slots})


def select_kernel(sizes, owner_hbm, slab_hbm, col_hbm, grad_hbm, *refs):
    blocks, owners, cap, x_size, z_size, core_size, y_size, cols, side = sizes
    tiers = capacities(x_size * core_size * cap)
    send_refs, refs = refs[: len(tiers)], refs[len(tiers) :]
    plan_ref, tier_ref, owner_ref, slab_ref, col_ref, grad_ref, pack_ref = refs[:7]
    count_ref, fill_ref, sems = refs[7:]
    stride = pack_ref.shape[1]
    copies = [
        pltpu.make_async_copy(source, target, sems.at[i])
        for i, (source, target) in enumerate(
            ((owner_hbm, owner_ref), (slab_hbm, slab_ref), (col_hbm, col_ref), (grad_hbm, grad_ref))
        )
    ]
    for copy in copies:
        copy.start()

    def clear(o, carry):
        count_ref[o] = 0
        return carry

    lax.fori_loop(0, owners, clear, 0, unroll=16)
    for z in range(z_size):
        fill_ref[z] = 0
    for s in range(stride):
        plan_ref[blocks + s] = y_size - 1
    plan_ref[blocks + 2 * stride] = lax.axis_index("y")
    z_here = lax.axis_index("z")
    for copy in copies[:3]:
        copy.wait()

    def assign(k, carry):
        o = owner_ref[k]
        rank = count_ref[o]
        count_ref[o] = rank + 1
        core = o & (core_size - 1)
        z = (o >> log2(core_size)) & (z_size - 1)
        x = o >> (log2(core_size) + log2(z_size))
        spot = fill_ref[z]
        fill_ref[z] = spot + 1
        tile = slab_ref[k] * cols + (col_ref[k] >> log2(side))
        plan_ref[tile] = z * stride + spot
        slot = (x * core_size + core) * y_size + rank
        plan_ref[spot + jnp.where(z == z_here, blocks, blocks + stride)] = slot
        return carry

    lax.fori_loop(0, blocks, assign, 0, unroll=8)
    copies[3].wait()

    def move(t, carry):
        code = plan_ref[t]
        pack_ref[code >> log2(stride), code & (stride - 1)] = grad_ref[t]
        return carry

    lax.fori_loop(0, blocks, move, 0, unroll=8)
    most = fill_ref[0]
    for z in range(1, z_size):
        most = jnp.maximum(most, fill_ref[z])
    tier = jnp.int32(len(tiers) - 1)
    for i in range(len(tiers) - 2, -1, -1):
        tier = jnp.where(most <= tiers[i], i, tier)
    tier_ref[0] = tier
    for i, send_ref in enumerate(send_refs):

        @pl.when(tier == i)
        def _():
            copy = pltpu.make_async_copy(pack_ref.at[:, : tiers[i]], send_ref, sems.at[4])
            copy.start()
            copy.wait()


def forward_kernel(cap, blocks, plan_ref, in_ref, *refs):
    out_ref = refs[-1]
    planes, y_size = out_ref.shape[:2]
    for p in range(planes):
        out_ref[p, :cap] = jnp.zeros_like(out_ref[p, :cap])
    for spot in range(in_ref.shape[1]):
        slot = plan_ref[blocks + spot]
        out_ref[slot >> log2(y_size), slot & (y_size - 1)] = in_ref[:, spot]


def backward_kernel(blocks, plan_ref, in_ref, after_ref, out_ref):
    y_size = in_ref.shape[1]
    for spot in range(out_ref.shape[1]):
        slot = plan_ref[blocks + spot]
        out_ref[:, spot] = in_ref[slot >> log2(y_size), slot & (y_size - 1)]


def around(position, size):
    return position & (size - 1)


def roots_kernel(plan_ref, left_ref, right_ref, *out_refs):
    parts = len(out_refs)
    quarter = left_ref.shape[1]
    for d, out_ref in enumerate(out_refs):
        s = jnp.minimum(around(plan_ref[plan_ref.shape[0] - 1] + d, parts), left_ref.shape[0] - 1)
        left = left_ref[s].astype(F32)
        right = right_ref[s].astype(F32)
        for j in range(parts):
            out_ref[j] = left[:, j * quarter : (j + 1) * quarter]
            out_ref[parts + j] = right[j * quarter : (j + 1) * quarter]


def split(value):
    high = value.astype(BF16)
    return high, (value - high.astype(F32)).astype(BF16)


def dot(a, b, a_dim, b_dim):
    return lax.dot_general(a, b, (((a_dim,), (b_dim,)), ((), ())), preferred_element_type=F32)


def tiles(shape):
    x_size, core_size, parts, z_size, rows, width = shape
    for x in range(x_size):
        for c in range(core_size):
            for q in range(parts):
                spot = (slice(x * z_size, (x + 1) * z_size), slice(c * rows, (c + 1) * rows))
                yield (x, c, q), spot + (slice(q * width, (q + 1) * width),)


def direction_kernel(plan_ref, in_ref, *refs):
    parts, width = in_ref.shape[2], in_ref.shape[5]
    pieces, refs = refs[:parts], refs[parts:]
    out_hbm, block_ref, left_ref, right_ref, result_ref, out_ref, sems = refs
    side = parts * width
    for part, spot in tiles(in_ref.shape):
        block_ref[spot] = in_ref[part]
    for d, piece in enumerate(pieces):
        q = around(plan_ref[plan_ref.shape[0] - 1] - d, parts)
        for j in range(parts):
            left_ref[pl.ds(q * width, width), j * width : (j + 1) * width] = piece[j].astype(BF16)
            right_ref[q, j * width : (j + 1) * width, :] = piece[parts + j].astype(BF16)
    high, low = split(block_ref[...].reshape(side, side))
    left = left_ref[...]
    half = parts // 2
    copies = []
    for h in range(2):
        columns = range(h * half, (h + 1) * half)
        right = jnp.concatenate([right_ref[q] for q in columns], axis=1)
        product = dot(high, right, 1, 0) + dot(low, right, 1, 0)
        result = dot(left, jnp.concatenate(split(product), axis=1), 1, 0)
        result = result[:, : half * width] + result[:, half * width :]
        result_ref[:, :, h * half * width : (h + 1) * half * width] = result.reshape(
            result_ref.shape[:2] + (half * width,)
        )
        for part, spot in tiles(in_ref.shape):
            if part[2] in columns:
                out_ref[part] = result_ref[spot]
        some = (slice(None), slice(None), pl.ds(h * half, half))
        copies.append(pltpu.make_async_copy(out_ref.at[some], out_hbm.at[some], sems.at[h]))
        copies[-1].start()
    for copy in copies:
        copy.wait()


def grams_kernel(plan_ref, in_ref, after_ref, *refs):
    out_refs, (block_ref, gram_ref) = refs[:-2], refs[-2:]
    parts = len(out_refs)
    quarter = out_refs[0].shape[1]
    side = block_ref.shape[2]
    for part, spot in tiles(in_ref.shape):
        block_ref[spot] = in_ref[part]
    high, low = split(block_ref[...].reshape(side, side))
    for i, dim in enumerate((1, 0)):
        gram_ref[i] = dot(high, high, dim, dim) + (dot(high, low, dim, dim) + dot(low, high, dim, dim))
    for d, out_ref in enumerate(out_refs):
        q = around(plan_ref[plan_ref.shape[0] - 1] + d, parts)
        out_ref[...] = gram_ref[:, pl.ds(q * quarter, quarter), :]


def finish_kernel(plan_ref, back_ref, left_hbm, right_hbm, *refs):
    parts = len(refs) - 7
    pieces, refs = refs[:parts], refs[parts:]
    placed_hbm, left_out, right_out, placed_ref, left_ref, right_ref, sems = refs
    blocks = placed_ref.shape[0]
    bits = log2(STRIDE)
    loads = [
        pltpu.make_async_copy(left_hbm, left_ref, sems.at[0]),
        pltpu.make_async_copy(right_hbm, right_ref, sems.at[1]),
    ]
    for copy in loads:
        copy.start()

    def step(t, carry):
        code = plan_ref[t]
        placed_ref[t] = back_ref[code >> bits, code & (STRIDE - 1)]
        return carry

    lax.fori_loop(0, blocks, step, 0, unroll=8)
    stores = [
        pltpu.make_async_copy(placed_ref, placed_hbm, sems.at[2]),
        pltpu.make_async_copy(left_ref, left_out, sems.at[3]),
        pltpu.make_async_copy(right_ref, right_out, sems.at[4]),
    ]
    stores[0].start()
    for i, ref in enumerate((left_ref, right_ref)):
        loads[i].wait()
        for d, piece in enumerate(pieces):
            s = around(plan_ref[plan_ref.shape[0] - 1] - d, parts)

            @pl.when(s < ref.shape[0])
            def _():
                ref[s] = BETA * ref[s] + (1.0 - BETA) * piece[i]

        stores[1 + i].start()
    for copy in stores:
        copy.wait()


def exchange(value, axes):
    return lax.all_to_all(value, axes, split_axis=0, concat_axis=0, tiled=True)


def spread(pieces):
    size = len(pieces)
    turn = lambda d: [(i, (i + d) % size) for i in range(size)]
    return [pieces[0]] + [lax.ppermute(pieces[d], "y", turn(d)) for d in range(1, size)]


def shape(*dims):
    return jax.ShapeDtypeStruct(dims, F32)


def step(index, blocks, plan, sends, left_factor, right_factor, left_root, right_root):
    x_size, z_size = lax.axis_size("x"), lax.axis_size("z")
    core_size, y_size = lax.axis_size("core"), lax.axis_size("y")
    planes = x_size * core_size
    cap, quarter, side = left_factor.shape
    send = sends[index]
    _, capacity, rows, width = send.shape
    cube = side * side * side * 2
    any_spec = pl.BlockSpec(memory_space=pl.ANY)

    roots = spread(
        call(
            roots_kernel,
            "roots",
            (shape(2 * y_size, quarter, quarter),) * y_size,
            (VMEM_SPEC,) * y_size,
            [SMEM_SPEC, VMEM_SPEC, VMEM_SPEC],
        )(plan, left_root, right_root)
    )

    moved = exchange(send, "z")
    moved = call(
        functools.partial(forward_kernel, cap, blocks),
        "forward",
        shape(planes, y_size, z_size, rows, width),
        VMEM_SPEC,
        [SMEM_SPEC, VMEM_SPEC] + [pl.BlockSpec(memory_space=pl.ANY)] * y_size,
    )(plan, moved, *roots)
    moved = exchange(moved.reshape(planes * y_size, z_size, rows, width), ("x", "core", "y"))

    moved = moved.reshape(x_size, core_size, y_size, z_size, rows, width)
    whole = pltpu.VMEM((x_size * z_size, core_size * rows, side), F32)
    directions = call(
        direction_kernel,
        "direction",
        shape(*moved.shape),
        any_spec,
        [SMEM_SPEC, VMEM_SPEC] + [VMEM_SPEC] * y_size,
        [
            whole,
            pltpu.VMEM((side, side), BF16),
            pltpu.VMEM((y_size, side, width), BF16),
            whole,
            pltpu.VMEM(moved.shape, F32),
            pltpu.SemaphoreType.DMA((2,)),
        ],
        flops=4 * cube,
        moved=6_000_000,
    )(plan, moved, *roots)

    grams = spread(
        call(
            grams_kernel,
            "grams",
            (shape(2, quarter, side),) * y_size,
            (VMEM_SPEC,) * y_size,
            [SMEM_SPEC, VMEM_SPEC, any_spec],
            [whole, pltpu.VMEM((2, side, side), F32)],
            flops=6 * cube,
            moved=5_000_000,
        )(plan, moved, directions)
    )
    back = exchange(directions.reshape(planes * y_size, z_size, rows, width), ("x", "core", "y"))
    back = call(
        functools.partial(backward_kernel, blocks),
        "backward",
        shape(z_size, capacity, rows, width),
        VMEM_SPEC,
        [SMEM_SPEC, VMEM_SPEC, pl.BlockSpec(memory_space=pl.ANY)],
    )(plan, back.reshape(planes, y_size, z_size, rows, width), grams[0])
    back = exchange(back, "z")

    factor = pltpu.VMEM(left_factor.shape, F32)
    return call(
        finish_kernel,
        "finish",
        (shape(blocks, rows, width), shape(*left_factor.shape), shape(*right_factor.shape)),
        (any_spec,) * 3,
        [SMEM_SPEC, VMEM_SPEC, any_spec, any_spec] + [VMEM_SPEC] * y_size,
        [pltpu.VMEM((blocks, rows, width), F32), factor, factor, pltpu.SemaphoreType.DMA((5,))],
        moved=6_000_000,
    )(plan, back, left_factor, right_factor, *grams)


def per_device(
    gradient, block_owner, block_slab, block_col, left_factor, right_factor, left_root, right_root
):
    x_size, z_size = lax.axis_size("x"), lax.axis_size("z")
    core_size, y_size = lax.axis_size("core"), lax.axis_size("y")
    owners = x_size * z_size * core_size
    cap, quarter, side = left_factor.shape
    slabs, rows, cols, width = gradient.shape
    blocks = block_owner.shape[0]
    tiers = capacities(x_size * core_size * cap)
    assert tiers[-1] <= STRIDE and cap < y_size
    index = lambda size: jax.ShapeDtypeStruct((size,), jnp.int32)
    any_spec = pl.BlockSpec(memory_space=pl.ANY)

    sizes = (blocks, owners, cap, x_size, z_size, core_size, y_size, cols, side)
    *sends, plan, tier = call(
        functools.partial(select_kernel, sizes),
        "select",
        tuple(shape(z_size, capacity, rows, width) for capacity in tiers)
        + (index(blocks + 2 * STRIDE + 1), index(1)),
        (any_spec,) * len(tiers) + (SMEM_SPEC,) * 2,
        [any_spec] * 4,
        [pltpu.SMEM((blocks,), jnp.int32)] * 3
        + [pltpu.VMEM((blocks, rows, width), F32), pltpu.VMEM((z_size, STRIDE, rows, width), F32)]
        + [pltpu.SMEM((owners,), jnp.int32), pltpu.SMEM((z_size,), jnp.int32), pltpu.SemaphoreType.DMA((5,))],
        moved=3_000_000,
        vmem=63 * 1024 * 1024,
    )(
        block_owner,
        block_slab,
        block_col,
        gradient.transpose(0, 2, 1, 3).reshape(blocks, rows, width),
    )
    placed, left_new, right_new = lax.switch(
        tier[0],
        [functools.partial(step, i, blocks) for i in range(len(tiers))],
        plan,
        sends,
        left_factor,
        right_factor,
        left_root,
        right_root,
    )
    placed = placed.reshape(slabs, cols, rows, width).transpose(0, 2, 1, 3)
    return placed, left_new, right_new


def solution(mesh, sizes=(4, 16, 2, 4)):
    fine = Mesh(mesh.devices.reshape(sizes), ("x", "z", "core", "y"))
    dp = ("x", "z", "core")
    return jax.shard_map(
        per_device,
        mesh=fine,
        in_specs=(
            P(None, dp, None, "y"),
            P(),
            P(),
            P(),
            P(dp, "y", None),
            P(dp, "y", None),
            P(dp, "y", None),
            P(dp, None, "y"),
        ),
        out_specs=(P(None, dp, None, "y"), P(dp, "y", None), P(dp, "y", None)),
        check_vma=False,
    )
```

```python
import functools

import jax
import jax.numpy as jnp
from jax import lax
from jax.experimental import pallas as pl
from jax.experimental.pallas import tpu as pltpu
from jax.sharding import Mesh
from jax.sharding import PartitionSpec as P

BETA = 0.95
STRIDE = 32
VMEM_BYTES = 24 * 1024 * 1024
F32 = jnp.float32
BF16 = jnp.bfloat16
SMEM_SPEC = pl.BlockSpec(memory_space=pltpu.SMEM)
VMEM_SPEC = pl.BlockSpec(memory_space=pltpu.VMEM)


def call(body, name, out_shape, out_specs, in_specs, scratch=(), flops=0, moved=1_000_000, vmem=VMEM_BYTES):
    return pl.pallas_call(
        body,
        out_shape=out_shape,
        in_specs=in_specs,
        out_specs=out_specs,
        scratch_shapes=list(scratch),
        compiler_params=pltpu.CompilerParams(vmem_limit_bytes=vmem),
        cost_estimate=pl.CostEstimate(flops=flops, bytes_accessed=moved, transcendentals=0),
        name=name,
    )


def log2(size):
    return size.bit_length() - 1


def capacities(plane_slots):
    return sorted({plane_slots * 3 // 4, plane_slots * 5 // 6, plane_slots})


def select_kernel(sizes, owner_hbm, slab_hbm, col_hbm, grad_hbm, *refs):
    blocks, owners, cap, x_size, z_size, core_size, y_size, cols, side = sizes
    tiers = capacities(x_size * core_size * cap)
    send_refs, refs = refs[: len(tiers)], refs[len(tiers) :]
    plan_ref, tier_ref, owner_ref, slab_ref, col_ref, grad_ref, pack_ref = refs[:7]
    count_ref, fill_ref, sems = refs[7:]
    stride = pack_ref.shape[1]
    copies = [
        pltpu.make_async_copy(source, target, sems.at[i])
        for i, (source, target) in enumerate(
            ((owner_hbm, owner_ref), (slab_hbm, slab_ref), (col_hbm, col_ref), (grad_hbm, grad_ref))
        )
    ]
    for copy in copies:
        copy.start()

    def clear(o, carry):
        count_ref[o] = 0
        return carry

    lax.fori_loop(0, owners, clear, 0, unroll=16)
    for z in range(z_size):
        fill_ref[z] = 0
    for s in range(stride):
        plan_ref[blocks + s] = y_size - 1
    plan_ref[blocks + 2 * stride] = lax.axis_index("y")
    z_here = lax.axis_index("z")
    for copy in copies:
        copy.wait()

    def move(k, carry):
        o = owner_ref[k]
        rank = count_ref[o]
        count_ref[o] = rank + 1
        core = o & (core_size - 1)
        z = (o >> log2(core_size)) & (z_size - 1)
        x = o >> (log2(core_size) + log2(z_size))
        spot = fill_ref[z]
        fill_ref[z] = spot + 1
        tile = slab_ref[k] * cols + (col_ref[k] >> log2(side))
        plan_ref[tile] = z * stride + spot
        slot = (x * core_size + core) * y_size + rank
        plan_ref[spot + jnp.where(z == z_here, blocks, blocks + stride)] = slot
        pack_ref[z, spot] = grad_ref[tile]
        return carry

    lax.fori_loop(0, blocks, move, 0, unroll=24)
    most = fill_ref[0]
    for z in range(1, z_size):
        most = jnp.maximum(most, fill_ref[z])
    tier = jnp.int32(len(tiers) - 1)
    for i in range(len(tiers) - 2, -1, -1):
        tier = jnp.where(most <= tiers[i], i, tier)
    tier_ref[0] = tier
    for i, send_ref in enumerate(send_refs):

        @pl.when(tier == i)
        def _():
            copy = pltpu.make_async_copy(pack_ref.at[:, : tiers[i]], send_ref, sems.at[4])
            copy.start()
            copy.wait()


def forward_kernel(cap, blocks, plan_ref, in_ref, *refs):
    out_ref = refs[-1]
    planes, y_size = out_ref.shape[:2]
    for p in range(planes):
        out_ref[p, :cap] = jnp.zeros_like(out_ref[p, :cap])
    for spot in range(in_ref.shape[1]):
        slot = plan_ref[blocks + spot]
        out_ref[slot >> log2(y_size), slot & (y_size - 1)] = in_ref[:, spot]


def backward_kernel(blocks, plan_ref, in_ref, after_ref, out_ref):
    y_size = in_ref.shape[1]
    for spot in range(out_ref.shape[1]):
        slot = plan_ref[blocks + spot]
        out_ref[:, spot] = in_ref[slot >> log2(y_size), slot & (y_size - 1)]


def around(position, size):
    return position & (size - 1)


def roots_kernel(plan_ref, left_ref, right_ref, *out_refs):
    parts = len(out_refs)
    quarter = left_ref.shape[1]
    for d, out_ref in enumerate(out_refs):
        s = jnp.minimum(around(plan_ref[plan_ref.shape[0] - 1] + d, parts), left_ref.shape[0] - 1)
        left = left_ref[s].astype(F32)
        right = right_ref[s].astype(F32)
        for j in range(parts):
            out_ref[j] = left[:, j * quarter : (j + 1) * quarter]
            out_ref[parts + j] = right[j * quarter : (j + 1) * quarter]


def split(value):
    high = value.astype(BF16)
    return high, (value - high.astype(F32)).astype(BF16)


def dot(a, b, a_dim, b_dim):
    return lax.dot_general(a, b, (((a_dim,), (b_dim,)), ((), ())), preferred_element_type=F32)


def tiles(shape):
    x_size, core_size, parts, z_size, rows, width = shape
    for x in range(x_size):
        for c in range(core_size):
            for q in range(parts):
                spot = (slice(x * z_size, (x + 1) * z_size), slice(c * rows, (c + 1) * rows))
                yield (x, c, q), spot + (slice(q * width, (q + 1) * width),)


def direction_kernel(plan_ref, in_ref, *refs):
    parts, width = in_ref.shape[2], in_ref.shape[5]
    pieces, (out_ref, block_ref, left_ref, right_ref, result_ref) = refs[:parts], refs[parts:]
    side = parts * width
    for part, spot in tiles(in_ref.shape):
        block_ref[spot] = in_ref[part]
    for d, piece in enumerate(pieces):
        q = around(plan_ref[plan_ref.shape[0] - 1] - d, parts)
        for j in range(parts):
            left_ref[pl.ds(q * width, width), j * width : (j + 1) * width] = piece[j].astype(BF16)
            right_ref[q, j * width : (j + 1) * width, :] = piece[parts + j].astype(BF16)
    high, low = split(block_ref[...].reshape(side, side))
    right = jnp.concatenate([right_ref[q] for q in range(parts)], axis=1)
    product = dot(high, right, 1, 0) + dot(low, right, 1, 0)
    high, low = split(product)
    left = left_ref[...]
    result_ref[...] = (dot(left, high, 1, 0) + dot(left, low, 1, 0)).reshape(result_ref.shape)
    for part, spot in tiles(in_ref.shape):
        out_ref[part] = result_ref[spot]


def grams_kernel(plan_ref, in_ref, after_ref, *refs):
    out_refs, (block_ref, gram_ref) = refs[:-2], refs[-2:]
    parts = len(out_refs)
    quarter = out_refs[0].shape[1]
    side = block_ref.shape[2]
    for part, spot in tiles(in_ref.shape):
        block_ref[spot] = in_ref[part]
    high, low = split(block_ref[...].reshape(side, side))
    for i, dim in enumerate((1, 0)):
        gram_ref[i] = dot(high, high, dim, dim) + (dot(high, low, dim, dim) + dot(low, high, dim, dim))
    for d, out_ref in enumerate(out_refs):
        q = around(plan_ref[plan_ref.shape[0] - 1] + d, parts)
        out_ref[...] = gram_ref[:, pl.ds(q * quarter, quarter), :]


def finish_kernel(plan_ref, back_ref, left_hbm, right_hbm, *refs):
    parts = len(refs) - 7
    pieces, refs = refs[:parts], refs[parts:]
    placed_hbm, left_out, right_out, placed_ref, left_ref, right_ref, sems = refs
    blocks = placed_ref.shape[0]
    bits = log2(STRIDE)
    loads = [
        pltpu.make_async_copy(left_hbm, left_ref, sems.at[0]),
        pltpu.make_async_copy(right_hbm, right_ref, sems.at[1]),
    ]
    for copy in loads:
        copy.start()

    def step(t, carry):
        code = plan_ref[t]
        placed_ref[t] = back_ref[code >> bits, code & (STRIDE - 1)]
        return carry

    lax.fori_loop(0, blocks, step, 0, unroll=8)
    stores = [
        pltpu.make_async_copy(placed_ref, placed_hbm, sems.at[2]),
        pltpu.make_async_copy(left_ref, left_out, sems.at[3]),
        pltpu.make_async_copy(right_ref, right_out, sems.at[4]),
    ]
    stores[0].start()
    for i, ref in enumerate((left_ref, right_ref)):
        loads[i].wait()
        for d, piece in enumerate(pieces):
            s = around(plan_ref[plan_ref.shape[0] - 1] - d, parts)

            @pl.when(s < ref.shape[0])
            def _():
                ref[s] = BETA * ref[s] + (1.0 - BETA) * piece[i]

        stores[1 + i].start()
    for copy in stores:
        copy.wait()


def exchange(value, axes):
    return lax.all_to_all(value, axes, split_axis=0, concat_axis=0, tiled=True)


def spread(pieces):
    size = len(pieces)
    turn = lambda d: [(i, (i + d) % size) for i in range(size)]
    far_first = sorted(range(1, size), key=lambda d: -min(d, size - d))
    moved = {d: lax.ppermute(pieces[d], "y", turn(d)) for d in far_first}
    return [pieces[0]] + [moved[d] for d in range(1, size)]


def shape(*dims):
    return jax.ShapeDtypeStruct(dims, F32)


def step(index, blocks, plan, sends, left_factor, right_factor, left_root, right_root):
    x_size, z_size = lax.axis_size("x"), lax.axis_size("z")
    core_size, y_size = lax.axis_size("core"), lax.axis_size("y")
    planes = x_size * core_size
    cap, quarter, side = left_factor.shape
    send = sends[index]
    _, capacity, rows, width = send.shape
    cube = side * side * side * 2
    any_spec = pl.BlockSpec(memory_space=pl.ANY)

    roots = spread(
        call(
            roots_kernel,
            "roots",
            (shape(2 * y_size, quarter, quarter),) * y_size,
            (VMEM_SPEC,) * y_size,
            [SMEM_SPEC, VMEM_SPEC, VMEM_SPEC],
        )(plan, left_root, right_root)
    )

    moved = exchange(send, "z")
    moved = call(
        functools.partial(forward_kernel, cap, blocks),
        "forward",
        shape(planes, y_size, z_size, rows, width),
        VMEM_SPEC,
        [SMEM_SPEC, VMEM_SPEC] + [pl.BlockSpec(memory_space=pl.ANY)] * y_size,
    )(plan, moved, *roots)
    moved = exchange(moved.reshape(planes * y_size, z_size, rows, width), ("x", "core", "y"))

    moved = moved.reshape(x_size, core_size, y_size, z_size, rows, width)
    whole = pltpu.VMEM((x_size * z_size, core_size * rows, side), F32)
    directions = call(
        direction_kernel,
        "direction",
        shape(*moved.shape),
        VMEM_SPEC,
        [SMEM_SPEC, VMEM_SPEC] + [VMEM_SPEC] * y_size,
        [
            whole,
            pltpu.VMEM((side, side), BF16),
            pltpu.VMEM((y_size, side, width), BF16),
            whole,
        ],
        flops=4 * cube,
        moved=6_000_000,
    )(plan, moved, *roots)

    grams = spread(
        call(
            grams_kernel,
            "grams",
            (shape(2, quarter, side),) * y_size,
            (VMEM_SPEC,) * y_size,
            [SMEM_SPEC, VMEM_SPEC, any_spec],
            [whole, pltpu.VMEM((2, side, side), F32)],
            flops=6 * cube,
            moved=5_000_000,
        )(plan, moved, directions)
    )
    back = exchange(directions.reshape(planes * y_size, z_size, rows, width), ("x", "core", "y"))
    back = call(
        functools.partial(backward_kernel, blocks),
        "backward",
        shape(z_size, capacity, rows, width),
        VMEM_SPEC,
        [SMEM_SPEC, VMEM_SPEC, pl.BlockSpec(memory_space=pl.ANY)],
    )(plan, back.reshape(planes, y_size, z_size, rows, width), grams[0])
    back = exchange(back, "z")

    factor = pltpu.VMEM(left_factor.shape, F32)
    return call(
        finish_kernel,
        "finish",
        (shape(blocks, rows, width), shape(*left_factor.shape), shape(*right_factor.shape)),
        (any_spec,) * 3,
        [SMEM_SPEC, VMEM_SPEC, any_spec, any_spec] + [VMEM_SPEC] * y_size,
        [pltpu.VMEM((blocks, rows, width), F32), factor, factor, pltpu.SemaphoreType.DMA((5,))],
        moved=6_000_000,
    )(plan, back, left_factor, right_factor, *grams)


def per_device(
    gradient, block_owner, block_slab, block_col, left_factor, right_factor, left_root, right_root
):
    x_size, z_size = lax.axis_size("x"), lax.axis_size("z")
    core_size, y_size = lax.axis_size("core"), lax.axis_size("y")
    owners = x_size * z_size * core_size
    cap, quarter, side = left_factor.shape
    slabs, rows, cols, width = gradient.shape
    blocks = block_owner.shape[0]
    tiers = capacities(x_size * core_size * cap)
    assert tiers[-1] <= STRIDE and cap < y_size
    index = lambda size: jax.ShapeDtypeStruct((size,), jnp.int32)
    any_spec = pl.BlockSpec(memory_space=pl.ANY)

    sizes = (blocks, owners, cap, x_size, z_size, core_size, y_size, cols, side)
    *sends, plan, tier = call(
        functools.partial(select_kernel, sizes),
        "select",
        tuple(shape(z_size, capacity, rows, width) for capacity in tiers)
        + (index(blocks + 2 * STRIDE + 1), index(1)),
        (any_spec,) * len(tiers) + (SMEM_SPEC,) * 2,
        [any_spec] * 4,
        [pltpu.SMEM((blocks,), jnp.int32)] * 3
        + [pltpu.VMEM((blocks, rows, width), F32), pltpu.VMEM((z_size, STRIDE, rows, width), F32)]
        + [pltpu.SMEM((owners,), jnp.int32), pltpu.SMEM((z_size,), jnp.int32), pltpu.SemaphoreType.DMA((5,))],
        moved=3_000_000,
        vmem=63 * 1024 * 1024,
    )(
        block_owner,
        block_slab,
        block_col,
        gradient.transpose(0, 2, 1, 3).reshape(blocks, rows, width),
    )
    placed, left_new, right_new = lax.switch(
        tier[0],
        [functools.partial(step, i, blocks) for i in range(len(tiers))],
        plan,
        sends,
        left_factor,
        right_factor,
        left_root,
        right_root,
    )
    placed = placed.reshape(slabs, cols, rows, width).transpose(0, 2, 1, 3)
    return placed, left_new, right_new


def solution(mesh, sizes=(4, 16, 2, 4)):
    fine = Mesh(mesh.devices.reshape(sizes), ("x", "z", "core", "y"))
    dp = ("x", "z", "core")
    return jax.shard_map(
        per_device,
        mesh=fine,
        in_specs=(
            P(None, dp, None, "y"),
            P(),
            P(),
            P(),
            P(dp, "y", None),
            P(dp, "y", None),
            P(dp, "y", None),
            P(dp, None, "y"),
        ),
        out_specs=(P(None, dp, None, "y"), P(dp, "y", None), P(dp, "y", None)),
        check_vma=False,
    )
```
